32 devices in a mesh: tm: 4 (over y, x), dp: 8 (over z, core).
Axes of the slice: x: 2, y: 2, z: 4, core: 2. Of those that a mesh axis runs over, the one named last changes fastest.
Arguments:
- clips: bfloat16 [8, 16, 32, 64, 128], P('dp', 'tm'), may hold values from -6 to 6
- weight: bfloat16 [3, 3, 3, 128, 256], replicated, may hold values from -0.109375 to 0.109375
- bias: float32 [256], replicated, may hold values from -3 to 3
- out_grad: bfloat16 [8, 8, 16, 32, 256], P('dp', 'tm'), may hold values from -6 to 6
Outputs:
- features: bfloat16 [8, 8, 16, 32, 256], P('dp', 'tm')
- clips_grad: bfloat16 [8, 16, 32, 64, 128], P('dp', 'tm')
- weight_grad: float32 [3, 3, 3, 128, 256], replicated
- bias_grad: float32 [256], replicated
The draws below stay inside these ranges and needn't reach their ends.
All inputs are finite; a program needn't handle non-finite values.
Results may differ from the reference program's by a relative error of at most 0.005.
Values may be sent and summed in bfloat16 or wider, within the bound.
A program may use at most 64 MiB of HBM per device.

```python
import math
import jax
import jax.numpy as jnp
from jax import lax

C_IN = 128
C_OUT = 256
ROWS = 32
COLS = 64
BATCH = 8
FRAMES = 16
OUTPOS = 32768


def level_of(key, extent, shards, smallest, high):
    def one(axis_at, shards_of):
        steps = jax.random.uniform(jax.random.fold_in(jax.random.fold_in(key, 6), axis_at), (shards_of,), jnp.float32, smallest / len(shards), high / len(shards))
        return jnp.repeat(jnp.exp(steps), extent[axis_at] // shards_of).reshape((-1,) + (1,) * (len(extent) - axis_at - 1))

    factor_of = one(*shards[0])
    for cut in shards[1:]:
        factor_of = factor_of * one(*cut)
    return factor_of


def normal_values(own_key, shape, deviation, limit, cuts=(), held_as=jnp.bfloat16):
    level = level_of(own_key, shape, cuts, -0.22, 0.18) if cuts else 1.0
    values = jax.random.normal(own_key, shape, jnp.float32) * deviation * level
    return jnp.minimum(jnp.maximum(values, -limit), limit).astype(held_as)


def setup_inputs(seed: int = 0) -> dict:
    arg_keys = jax.random.split(jax.random.key(seed), 5)
    return {
        "clips": normal_values(arg_keys[0], (BATCH, FRAMES, ROWS, COLS, C_IN), 1.0, 6.0, ((0, 8), (1, 4))),
        "weight": normal_values(arg_keys[1], (3, 3, 3, C_IN, C_OUT), (27 * C_IN) ** -0.5, 0.109375),
        "bias": normal_values(arg_keys[2], (C_OUT,), 0.5, 3.0, (), jnp.float32),
        "out_grad": normal_values(arg_keys[3], (BATCH, FRAMES // 2, ROWS // 2, COLS // 2, C_OUT), 1.0, 6.0, ((0, 8), (1, 4))),
    }


def conv_forward(padded, kernel):
    return lax.conv_general_dilated(padded, kernel, (2, 2, 2), ((0, 0), (1, 1), (1, 1)), dimension_numbers=('NDHWC', 'DHWIO', 'NDHWC'), precision=lax.Precision.HIGHEST)

def reference(clips, weight, bias, out_grad):
    kernel = weight.astype(jnp.float32)

    def one_clip(pair):
        frames_in, grad_in = pair
        padded = jnp.pad(frames_in.astype(jnp.float32)[None], ((0, 0), (2, 0), (0, 0), (0, 0), (0, 0)))
        pre = conv_forward(padded, kernel)[0] + bias
        sig = jax.nn.sigmoid(pre)
        feats = (pre * sig).astype(jnp.bfloat16)
        pre_grad = (grad_in.astype(jnp.float32) * (sig * (1.0 + pre * (1.0 - sig)))).astype(jnp.bfloat16)
        _, pull = jax.vjp(conv_forward, padded, kernel)
        padded_grad, kernel_grad = pull(pre_grad.astype(jnp.float32)[None])
        input_grad = padded_grad[0, 2:].astype(jnp.bfloat16)
        bias_part = lax.optimization_barrier(jnp.sum(pre_grad.astype(jnp.float32), axis=(0, 1, 2)))
        return (feats, input_grad, kernel_grad, bias_part)
    feats, input_grad, kernel_grads, bias_parts = lax.map(one_clip, (clips, out_grad))
    scale = 1.0 / math.sqrt(OUTPOS)
    weight_grad = lax.optimization_barrier(jnp.sum(kernel_grads, axis=0)) * scale
    bias_grad = lax.optimization_barrier(jnp.sum(bias_parts, axis=0)) * scale
    return (feats, input_grad, weight_grad, bias_grad)
```

```python
import functools
import math

import jax
import jax.numpy as jnp
from jax import lax
from jax.experimental import pallas as pl
from jax.experimental.pallas import tpu as pltpu
from jax.sharding import PartitionSpec as P

MESH = pl.DeviceIdType.MESH
BF = jnp.bfloat16
F32 = jnp.float32


def passed_along(value, axis, steps):
    count = lax.axis_size(axis)
    first, last = (max(0, -steps), min(count, count - steps))
    return lax.ppermute(value, axis, [(source, source + steps) for source in range(first, last)])


def sum_kernel(tms, zs, part, out, wire, got1, own1, send2, got2, own2, send3, got3, sems_s, sems_r):
    tm = lax.axis_index("tm")
    dp = lax.axis_index("dp")
    core = dp % 2
    z = dp // 2
    mate = dp + 1 - 2 * core
    half = part.shape[0] // 2
    quarter = half // tms
    piece = quarter // zs

    mates = [{"tm": tm, "dp": mate}]
    plane = [{"tm": (tm + d) % tms, "dp": dp} for d in range(1, tms)]
    line = [{"tm": tm, "dp": ((z + d) % zs) * 2 + core} for d in range(1, zs)]
    everyone = mates + plane + line

    barrier = pltpu.get_barrier_semaphore()
    for other in everyone:
        pl.semaphore_signal(barrier, inc=1, device_id=other, device_id_type=MESH)

    def rows(start, count):
        return pl.ds(pl.multiple_of(start, 16), count)

    wire[...] = part[rows((1 - core) * half, half), :].astype(BF)
    pl.semaphore_wait(barrier, len(everyone))

    def copy(src, dst, slot, to):
        made = pltpu.make_async_remote_copy(
            src_ref=src,
            dst_ref=dst,
            send_sem=sems_s.at[slot],
            recv_sem=sems_r.at[slot],
            device_id=to,
            device_id_type=MESH,
        )
        made.start()
        return made

    slot = 0
    first = copy(wire, got1, slot, mates[0])
    slot += 1
    first.wait()
    own1[...] = part[rows(core * half, half), :] + got1[...].astype(F32)
    send2[...] = own1[...].astype(BF)

    copies = []
    for d in range(1, tms):
        src = send2.at[rows(((tm + d) % tms) * quarter, quarter), :]
        copies.append(copy(src, got2.at[d - 1], slot, plane[d - 1]))
        slot += 1
    for made in copies:
        made.wait()
    total = own1[rows(tm * quarter, quarter), :]
    for d in range(1, tms):
        total = total + got2[d - 1].astype(F32)
    own2[...] = total
    send3[...] = total.astype(BF)

    copies = []
    for d in range(1, zs):
        src = send3.at[rows(((z + d) % zs) * piece, piece), :]
        copies.append(copy(src, got3.at[d - 1], slot, line[d - 1]))
        slot += 1
    for made in copies:
        made.wait()
    total = own2[rows(z * piece, piece), :]
    for d in range(1, zs):
        total = total + got3[d - 1].astype(F32)
    at3 = core * half + tm * quarter + z * piece
    out[rows(at3, piece), :] = total.astype(BF)

    for start, count, group in (
        (at3, piece, line),
        (core * half + tm * quarter, quarter, plane),
        (core * half, half, mates),
    ):
        copies = []
        for other in group:
            block = out.at[rows(start, count), :]
            copies.append(copy(block, block, slot, other))
            slot += 1
        for made in copies:
            made.wait()


def summed(part):
    tms = lax.axis_size("tm")
    zs = lax.axis_size("dp") // 2
    rows, cols = part.shape
    half = rows // 2
    quarter = half // tms
    piece = quarter // zs
    count = 2 * (1 + (tms - 1) + (zs - 1))
    return pl.pallas_call(
        functools.partial(sum_kernel, tms, zs),
        out_shape=jax.ShapeDtypeStruct((rows, cols), BF),
        in_specs=[pl.BlockSpec(memory_space=pltpu.VMEM)],
        out_specs=pl.BlockSpec(memory_space=pltpu.VMEM),
        scratch_shapes=[
            pltpu.VMEM((half, cols), BF),
            pltpu.VMEM((half, cols), BF),
            pltpu.VMEM((half, cols), F32),
            pltpu.VMEM((half, cols), BF),
            pltpu.VMEM((max(1, tms - 1), quarter, cols), BF),
            pltpu.VMEM((quarter, cols), F32),
            pltpu.VMEM((quarter, cols), BF),
            pltpu.VMEM((max(1, zs - 1), piece, cols), BF),
            pltpu.SemaphoreType.DMA((count,)),
            pltpu.SemaphoreType.DMA((count,)),
        ],
        compiler_params=pltpu.CompilerParams(
            collective_id=0, has_side_effects=True, vmem_limit_bytes=32 * 1024 * 1024
        ),
    )(part)


def forward_conv(frames, weight):
    return lax.conv_general_dilated(
        frames,
        weight,
        (2, 2, 2),
        ((0, 0), (1, 1), (1, 1)),
        dimension_numbers=("NDHWC", "DHWIO", "NDHWC"),
        preferred_element_type=F32,
    )


def back_conv(grads, weight, low, high):
    flipped = weight[::-1, ::-1, ::-1]
    return lax.conv_general_dilated(
        grads,
        flipped,
        (1, 1, 1),
        ((low, high), (1, 2), (1, 2)),
        lhs_dilation=(2, 2, 2),
        dimension_numbers=("NDHWC", "DHWOI", "NDHWC"),
        preferred_element_type=F32,
    )


def kernel_conv(clips, grads):
    return lax.conv_general_dilated(
        clips,
        grads,
        (1, 1, 1),
        ((2, 1), (1, 0), (1, 0)),
        rhs_dilation=(2, 2, 2),
        dimension_numbers=("CDHWN", "IDHWO", "DHWNC"),
        preferred_element_type=F32,
    )


def local(clips, weight, bias, out_grad):
    frames = clips.shape[1]
    spill = forward_conv(clips[:, frames - 2 :], weight[:2]).astype(BF)
    prior = passed_along(spill, "tm", 1)
    later_pre = forward_conv(clips[:, : frames - 1], weight)
    first_pre = forward_conv(clips[:, :1], weight[2:]) + prior.astype(F32)
    pre = jnp.concatenate([first_pre, later_pre], axis=1) + bias
    sig = jax.nn.sigmoid(pre)
    features = (pre * sig).astype(BF)
    pre_grad = (out_grad.astype(F32) * (sig * (1.0 + pre * (1.0 - sig)))).astype(BF)
    following = passed_along(pre_grad[:, :1], "tm", -1)
    grads = jnp.concatenate([pre_grad, following], axis=1)
    kernel_part = kernel_conv(clips, grads)
    bias_part = jnp.sum(pre_grad.astype(F32), axis=(0, 1, 2, 3))

    c_out = bias.shape[0]
    taps = kernel_part.size // c_out
    devices = lax.axis_size("tm") * lax.axis_size("dp")
    step = 16 * devices
    rows = -(-(taps + 2) // step) * step
    high = bias_part.astype(BF).astype(F32)
    tail = jnp.concatenate(
        [high[None], (bias_part - high)[None], jnp.zeros((rows - taps - 2, c_out), F32)]
    )
    total = summed(jnp.concatenate([kernel_part.reshape(taps, c_out), tail]))
    clips_grad = back_conv(grads, weight, 0, 1).astype(BF)

    positions = pre_grad.size // c_out * devices
    scale = 1.0 / math.sqrt(positions)
    kernel_grad = total[:taps].astype(F32).reshape(kernel_part.shape) * scale
    bias_sum = total[taps].astype(F32) + total[taps + 1].astype(F32)
    return (features, clips_grad, kernel_grad, bias_sum * scale)


def solution(mesh):
    in_specs = (P("dp", "tm", None, None, None), P(), P(), P("dp", "tm", None, None, None))
    out_specs = (P("dp", "tm", None, None, None), P("dp", "tm", None, None, None), P(), P())
    return jax.shard_map(local, mesh=mesh, in_specs=in_specs, out_specs=out_specs, check_vma=False)
```
